32 devices in a mesh: seq: 8 (over z, y), head: 4 (over x, core).
Axes of the slice: x: 2, y: 2, z: 4, core: 2. Of those that a mesh axis runs over, the one named last changes fastest.
Arguments:
- queries: bfloat16 [1024, 4096], P(('seq', 'head')), may hold values from -6 to 6
- key_vectors: bfloat16 [1024, 4096], P(('seq', 'head')), may hold values from -6 to 6
- value_vectors: bfloat16 [1024, 4096], P(('seq', 'head')), may hold values from -6 to 6
- out_cotangent: bfloat16 [1024, 4096], P(('seq', 'head')), may hold values from -6 to 6
- block_mask: int32 [8, 4], replicated, may hold values from 0 to 1, as said below
Outputs:
- attended: bfloat16 [1024, 4096], P(('seq', 'head'))
- query_grad: bfloat16 [1024, 4096], P(('seq', 'head'))
- key_grad: bfloat16 [1024, 4096], P(('seq', 'head'))
- value_grad: bfloat16 [1024, 4096], P(('seq', 'head'))
The draws below stay inside these ranges and needn't reach their ends.
Inputs may be any that keep to these rules, and one draw needn't show every extreme that they name: `block_mask`: column 0 is 1 in every row; entry [b, j] with j >= 1 is 0 where b < 2**(j-1).
All inputs are finite; a program needn't handle non-finite values.
Results may differ from the reference program's by a relative error of at most 0.035.
Values may be sent and summed in bfloat16 or wider, within the bound.
A program may use at most 64 MiB of HBM per device.

```python
import jax
import jax.numpy as jnp
from jax import lax

H = 32
DH = 128
D = 4096
BLK = 128
TOKENS = 1024
NB = 8
NOFF = 4


def drawn_pair(key):
    query_key = jax.random.fold_in(key, 101)
    key_key = jax.random.fold_in(key, 102)
    queries = 2.0 * jax.random.truncated_normal(query_key, -3.0, 3.0, (TOKENS, D), jnp.float32)
    keyrows = jax.random.truncated_normal(key_key, -4.0, 4.0, (TOKENS, D), jnp.float32)
    return (queries, keyrows)


def draw_queries(key, part):
    return drawn_pair(key)[0].astype(jnp.bfloat16)


def draw_key_vectors(key, part):
    return drawn_pair(key)[1].astype(jnp.bfloat16)


def draw_block_mask(key, part):
    coin_flips = jax.random.randint(jax.random.fold_in(key, 201), (NB, NOFF), 0, 4)
    column = jnp.arange(NOFF)[None, :]
    row_index = jnp.arange(NB)[:, None]
    distance = jnp.where(column == 0, 0, 2 ** jnp.maximum(column - 1, 0))
    sampled = jnp.where(coin_flips != 0, 1, 0)
    return jnp.where(column == 0, 1, jnp.where(row_index >= distance, sampled, 0)).astype(jnp.int32)


def level_of(key, extent, cuts, low, largest):
    loudness = 1.0
    for axis_at, parts in cuts:
        heights = jax.random.uniform(jax.random.fold_in(jax.random.fold_in(key, 6), axis_at), (parts,), jnp.float32, low / len(cuts), largest / len(cuts))
        loudness = loudness * jnp.repeat(jnp.exp(heights), extent[axis_at] // parts).reshape((-1,) + (1,) * (len(extent) - 1 - axis_at))
    return loudness


def scatter_about(own_key, shape, scale, bound, pieces=(), held_as=jnp.bfloat16):
    entries = scale * jax.random.normal(own_key, shape, jnp.float32)
    if pieces:
        entries = entries * level_of(own_key, shape, pieces, -0.22, 0.18)
    return jnp.clip(entries, -bound, bound).astype(held_as)


def setup_inputs(seed: int = 0) -> dict:
    seeds = jax.random.split(jax.random.key(seed), 6)
    return {
        "queries": draw_queries(jax.random.fold_in(seeds[5], 71), 0),
        "key_vectors": draw_key_vectors(jax.random.fold_in(seeds[5], 71), 0),
        "value_vectors": scatter_about(seeds[2], (TOKENS, D), 1.0, 6.0, ((0, 32),)),
        "out_cotangent": scatter_about(seeds[3], (TOKENS, D), 1.0, 6.0, ((0, 32),)),
        "block_mask": draw_block_mask(jax.random.fold_in(seeds[5], 71), 0),
    }


NEG = -1e30


def reference(queries, key_vectors, value_vectors, out_cotangent, block_mask):
    blocks = TOKENS // BLK
    offsets = [0] + [2 ** level for level in range(NOFF - 1)]
    score_scale = DH ** -0.5
    block_shape = (blocks, BLK, H, DH)
    query_blocks = queries.reshape(block_shape)
    key_blocks = key_vectors.reshape(block_shape)
    value_blocks = value_vectors.reshape(block_shape)
    grad_blocks = out_cotangent.reshape(block_shape)
    shift_table = jnp.array(offsets, dtype=jnp.int32)
    position = jnp.arange(BLK, dtype=jnp.int32)
    causal = position[None, :] <= position[:, None]
    later = jnp.arange(NOFF, dtype=jnp.int32)[None, :, None] > 0
    block_rows = jnp.arange(blocks, dtype=jnp.int32)

    def forward_block(block_row):
        sources = jnp.maximum(block_row - shift_table, 0).astype(jnp.int32)
        keys_here = key_blocks[sources].astype(jnp.float32)
        values_here = value_blocks[sources].astype(jnp.float32)
        query_here = query_blocks[block_row].astype(jnp.float32)
        scores = jnp.einsum('qhd,jkhd->hqjk', query_here, keys_here) * score_scale
        live = block_mask[block_row] == 1
        allowed = live[None, :, None] & (later | causal[:, None, :])
        scores = jnp.where(allowed[None], scores, NEG)
        row_max = jnp.max(scores, axis=(2, 3))
        row_total = jnp.sum(jnp.exp(scores - row_max[:, :, None, None]), axis=(2, 3))
        log_total = row_max + jnp.log(row_total)
        rounded = jnp.exp(scores - log_total[:, :, None, None]).astype(jnp.bfloat16)
        attended = jnp.einsum('hqjk,jkhd->qhd', rounded.astype(jnp.float32), values_here)
        return attended.astype(jnp.bfloat16), log_total

    attended_blocks, log_totals = lax.map(forward_block, block_rows)
    row_delta = jnp.einsum('bqhd,bqhd->bhq', grad_blocks.astype(jnp.float32), attended_blocks.astype(jnp.float32))

    query_grad = jnp.zeros(block_shape, jnp.float32)
    key_grad = jnp.zeros(block_shape, jnp.float32)
    value_grad = jnp.zeros(block_shape, jnp.float32)
    for column, offset in enumerate(offsets):
        def backward_block(block_row, column=column, offset=offset):
            source = jnp.maximum(block_row - offset, 0).astype(jnp.int32)
            key_here = key_blocks[source].astype(jnp.float32)
            value_here = value_blocks[source].astype(jnp.float32)
            query_here = query_blocks[block_row].astype(jnp.float32)
            grad_here = grad_blocks[block_row].astype(jnp.float32)
            scores = jnp.einsum('qhd,khd->hqk', query_here, key_here) * score_scale
            live = block_mask[block_row, column] == 1
            if offset == 0:
                allowed = live & causal
            else:
                allowed = live & jnp.ones((BLK, BLK), dtype=bool)
            scores = jnp.where(allowed[None], scores, NEG)
            weights = jnp.exp(scores - log_totals[block_row][:, :, None])
            rounded = weights.astype(jnp.bfloat16)
            grad_weights = jnp.einsum('qhd,khd->hqk', grad_here, value_here)
            grad_scores = (weights * (grad_weights - row_delta[block_row][:, :, None]) * score_scale).astype(jnp.bfloat16)
            query_term = jnp.einsum('hqk,khd->qhd', grad_scores.astype(jnp.float32), key_here)
            key_term = jnp.einsum('hqk,qhd->khd', grad_scores.astype(jnp.float32), query_here)
            value_term = jnp.einsum('hqk,qhd->khd', rounded.astype(jnp.float32), grad_here)
            return query_term, key_term, value_term

        query_terms, key_terms, value_terms = lax.map(backward_block, block_rows)
        query_grad = query_grad + query_terms
        key_grad = key_grad + jnp.roll(key_terms, -offset, axis=0)
        value_grad = value_grad + jnp.roll(value_terms, -offset, axis=0)

    flat = (TOKENS, H * DH)
    return (attended_blocks.reshape(flat),
            query_grad.astype(jnp.bfloat16).reshape(flat),
            key_grad.astype(jnp.bfloat16).reshape(flat),
            value_grad.astype(jnp.bfloat16).reshape(flat))
```

```python
import functools

import jax
import jax.numpy as jnp
from jax import lax
from jax.experimental import pallas as pl
from jax.experimental.pallas import tpu as pltpu
from jax.sharding import PartitionSpec as P

DH = 128
BLK = 128


NEG = -1e30


def from_behind(block, axis, distance):
    devices = range(lax.axis_size(axis))
    route = [(i - distance, i) for i in devices if i - distance in devices]
    return lax.ppermute(block, axis, route)


def pick_block(offset, blocks, own, arrived):
    if offset == 0:
        return own
    if offset <= blocks:
        joined = jnp.concatenate([arrived[1], own], axis=0)
        return joined[blocks - offset : 2 * blocks - offset]
    return arrived[offset // blocks]


def shards(queries, key_vectors, value_vectors, out_cotangent, block_mask):
    seq_count = lax.axis_size("seq")
    seq_index = lax.axis_index("seq")
    head_queries, head_keys, head_values, head_grads = (
        lax.all_to_all(queries, "head", split_axis=1, concat_axis=0, tiled=True),
        lax.all_to_all(key_vectors, "head", split_axis=1, concat_axis=0, tiled=True),
        lax.all_to_all(value_vectors, "head", split_axis=1, concat_axis=0, tiled=True),
        lax.all_to_all(out_cotangent, "head", split_axis=1, concat_axis=0, tiled=True),
    )
    patches = head_queries.shape[0]
    local_heads = head_queries.shape[1] // DH
    blocks = patches // BLK
    block_shape = (blocks, BLK, local_heads, DH)
    query_own = head_queries.reshape(block_shape)
    key_own = head_keys.reshape(block_shape)
    value_own = head_values.reshape(block_shape)
    grad_own = head_grads.reshape(block_shape)
    columns = block_mask.shape[1]
    offsets = [0] + [2**level for level in range(columns - 1)]
    distances = [2**level for level in range(seq_count.bit_length() - 1)]
    score_scale = DH ** (-0.5)
    my_mask = lax.dynamic_slice_in_dim(block_mask, seq_index * blocks, blocks, 0)
    arrived_keys = {}
    arrived_values = {}
    for distance in distances:
        moved = from_behind((key_own, value_own), "seq", distance)
        arrived_keys[distance] = moved[0]
        arrived_values[distance] = moved[1]
    keys_all = jnp.stack([pick_block(offset, blocks, key_own, arrived_keys) for offset in offsets])
    values_all = jnp.stack(
        [pick_block(offset, blocks, value_own, arrived_values) for offset in offsets]
    )
    position = jnp.arange(BLK)
    causal = position[None, :] <= position[:, None]
    later = jnp.arange(columns)[None, :, None] > 0
    allowed = (my_mask[:, None, None, :, None] == 1) & (
        later[None, None] | causal[None, None, :, None, :]
    )
    scores = (
        jnp.einsum("bqhd,jbkhd->bhqjk", query_own, keys_all, preferred_element_type=jnp.float32)
        * score_scale
    )
    scores = jnp.where(allowed, scores, NEG)
    row_max = jnp.max(scores, axis=(3, 4))
    row_total = jnp.sum(jnp.exp(scores - row_max[..., None, None]), axis=(3, 4))
    log_total = row_max + jnp.log(row_total)
    weights = jnp.exp(scores - log_total[..., None, None])
    rounded = weights.astype(jnp.bfloat16)
    attended = jnp.einsum(
        "bhqjk,jbkhd->bqhd", rounded, values_all, preferred_element_type=jnp.float32
    ).astype(jnp.bfloat16)
    attended_out = lax.all_to_all(
        attended.reshape(patches, local_heads * DH), "head", split_axis=0, concat_axis=1, tiled=True
    )
    row_delta = jnp.einsum("bqhd,bqhd->bhq", grad_own, attended, preferred_element_type=jnp.float32)
    grad_weights = jnp.einsum(
        "bqhd,jbkhd->bhqjk", grad_own, values_all, preferred_element_type=jnp.float32
    )
    grad_scores = (weights * (grad_weights - row_delta[..., None, None]) * score_scale).astype(
        jnp.bfloat16
    )
    query_grad = jnp.einsum(
        "bhqjk,jbkhd->bqhd", grad_scores, keys_all, preferred_element_type=jnp.float32
    ).astype(jnp.bfloat16)
    key_parts = jnp.einsum(
        "bhqjk,bqhd->jbkhd", grad_scores, query_own, preferred_element_type=jnp.float32
    )
    value_parts = jnp.einsum(
        "bhqjk,bqhd->jbkhd", rounded, grad_own, preferred_element_type=jnp.float32
    )
    key_grad = key_parts[0]
    value_grad = value_parts[0]
    near_keys = jnp.zeros((2 * blocks,) + block_shape[1:], jnp.float32)
    near_values = jnp.zeros((2 * blocks,) + block_shape[1:], jnp.float32)
    outgoing_keys = {}
    outgoing_values = {}
    for column in range(1, columns):
        offset = offsets[column]
        if offset <= blocks:
            padding = ((blocks - offset, offset), (0, 0), (0, 0), (0, 0))
            near_keys = jnp.pad(key_parts[column], padding)
            near_values = jnp.pad(value_parts[column], padding)
        else:
            outgoing_keys[offset // blocks] = key_parts[column]
            outgoing_values[offset // blocks] = value_parts[column]
    key_grad = key_grad + near_keys[blocks:]
    value_grad = value_grad + near_values[blocks:]
    outgoing_keys[1] = near_keys[:blocks]
    outgoing_values[1] = near_values[:blocks]
    for distance in distances:
        returned = (
            from_behind(outgoing_keys[distance].astype(jnp.bfloat16), "seq", -distance).astype(
                jnp.float32
            ),
            from_behind(outgoing_values[distance].astype(jnp.bfloat16), "seq", -distance).astype(
                jnp.float32
            ),
        )
        key_grad = key_grad + returned[0]
        value_grad = value_grad + returned[1]
    flat = (patches, local_heads * DH)
    grads_out = (
        lax.all_to_all(query_grad.reshape(flat), "head", split_axis=0, concat_axis=1, tiled=True),
        lax.all_to_all(
            key_grad.astype(jnp.bfloat16).reshape(flat),
            "head",
            split_axis=0,
            concat_axis=1,
            tiled=True,
        ),
        lax.all_to_all(
            value_grad.astype(jnp.bfloat16).reshape(flat),
            "head",
            split_axis=0,
            concat_axis=1,
            tiled=True,
        ),
    )
    return (attended_out, grads_out[0], grads_out[1], grads_out[2])


def rows_of(index, size):
    return pl.ds(pl.multiple_of(index * size, size), size)


def fused_kernel(
    seq_count,
    head_count,
    mask_ref,
    q_ref,
    k_ref,
    v_ref,
    g_ref,
    out_ref,
    dq_ref,
    dk_ref,
    dv_ref,
    outbound,
    inbound,
    results,
    landed,
    key_sum,
    value_sum,
    local_sem,
    send_one,
    recv_one,
    send_two,
    recv_two,
):
    devices = seq_count * head_count
    rows, width = q_ref.shape
    features = width // devices
    local_heads = features // DH
    blocks, columns = mask_ref.shape
    offsets = [0] + [2**level for level in range(columns - 1)]
    scale = DH ** (-0.5)
    me = lax.axis_index("seq") * head_count + lax.axis_index("head")

    def place(index):
        return (index // head_count, index % head_count)

    loads = [
        pltpu.make_async_copy(ref, outbound.at[i], local_sem.at[i])
        for i, ref in enumerate((q_ref, k_ref, v_ref, g_ref))
    ]
    for load in loads:
        load.start()

    barrier = pltpu.get_barrier_semaphore()

    def greet(step, carry):
        pl.semaphore_signal(
            barrier,
            inc=1,
            device_id=place((me + step) % devices),
            device_id_type=pl.DeviceIdType.MESH,
        )
        return carry

    lax.fori_loop(1, devices, greet, 0)
    for load in loads:
        load.wait()
    pl.semaphore_wait(barrier, devices - 1)

    def peer_of(step):
        turn = devices // 2 + (1 - 2 * (step % 2)) * ((step + 1) // 2)
        return (me + turn) % devices

    def first_copy(peer, slot):
        return pltpu.make_async_remote_copy(
            src_ref=outbound.at[:, :, rows_of(peer, features)],
            dst_ref=inbound.at[:, rows_of(slot, rows), :],
            send_sem=send_one.at[peer],
            recv_sem=recv_one.at[slot],
            device_id=place(peer),
            device_id_type=pl.DeviceIdType.MESH,
        )

    def second_copy(peer, slot):
        return pltpu.make_async_remote_copy(
            src_ref=results.at[:, rows_of(peer, rows), :],
            dst_ref=landed.at[:, :, rows_of(slot, features)],
            send_sem=send_two.at[peer],
            recv_sem=recv_two.at[slot],
            device_id=place(peer),
            device_id_type=pl.DeviceIdType.MESH,
        )

    def start_first(step, carry):
        first_copy(peer_of(step), me).start()
        return carry

    lax.fori_loop(0, devices - 1, start_first, 0)
    inbound[:, rows_of(me, rows), :] = outbound[:, :, rows_of(me, features)]

    def wait_first(step, carry):
        peer = peer_of(step)
        copy = first_copy(peer, peer)
        copy.wait_send()
        copy.wait_recv()
        return carry

    lax.fori_loop(0, devices - 1, wait_first, 0)

    query_at = lax.broadcasted_iota(jnp.int32, (BLK, BLK), 0)
    key_at = lax.broadcasted_iota(jnp.int32, (BLK, BLK), 1)
    causal = key_at <= query_at

    def dot(a, b, dims):
        return lax.dot_general(a, b, (dims, ((), ())), preferred_element_type=jnp.float32)

    def attend(block, carry):
        here = rows_of(block, BLK)
        sources = [rows_of(jnp.maximum(block - offset, 0), BLK) for offset in offsets]
        for head in range(local_heads):
            part = slice(head * DH, (head + 1) * DH)
            query = inbound[0, here, part]
            grad = inbound[3, here, part]
            keys = jnp.concatenate([inbound[1, source, part] for source in sources], axis=0)
            values = jnp.concatenate([inbound[2, source, part] for source in sources], axis=0)
            scores = dot(query, keys, ((1,), (1,))) * scale
            pieces = []
            for j in range(columns):
                live = mask_ref[block, j] == 1
                piece = scores[:, j * BLK : (j + 1) * BLK]
                if j == 0:
                    piece = jnp.where(causal, piece, NEG)
                pieces.append(jnp.where(live, piece, NEG))
            scores = jnp.concatenate(pieces, axis=1)
            row_max = jnp.max(scores, axis=1, keepdims=True)
            raised = jnp.exp(scores - row_max)
            total = jnp.sum(raised, axis=1, keepdims=True)
            weights = raised * (1.0 / total)
            rounded = weights.astype(jnp.bfloat16)
            attended = dot(rounded, values, ((1,), (0,))).astype(jnp.bfloat16)
            delta = jnp.sum(
                grad.astype(jnp.float32) * attended.astype(jnp.float32), axis=1, keepdims=True
            )
            grad_weights = dot(grad, values, ((1,), (1,)))
            grad_scores = (weights * (grad_weights - delta) * scale).astype(jnp.bfloat16)
            query_grad = dot(grad_scores, keys, ((1,), (0,))).astype(jnp.bfloat16)
            key_parts = dot(grad_scores, query, ((0,), (0,)))
            value_parts = dot(rounded, grad, ((0,), (0,)))
            results[0, here, part] = attended
            results[1, here, part] = query_grad
            key_sum[here, part] = key_parts[:BLK]
            value_sum[here, part] = value_parts[:BLK]
            for j in range(1, columns):
                piece = slice(j * BLK, (j + 1) * BLK)
                key_sum[sources[j], part] += key_parts[piece]
                value_sum[sources[j], part] += value_parts[piece]
        return carry

    lax.fori_loop(0, blocks, attend, 0)

    def finish(block, carry):
        here = rows_of(block, BLK)
        results[2, here, :] = key_sum[here, :].astype(jnp.bfloat16)
        results[3, here, :] = value_sum[here, :].astype(jnp.bfloat16)
        return carry

    lax.fori_loop(0, blocks, finish, 0)

    def start_second(step, carry):
        second_copy(peer_of(step), me).start()
        return carry

    lax.fori_loop(0, devices - 1, start_second, 0)
    landed[:, :, rows_of(me, features)] = results[:, rows_of(me, rows), :]

    def wait_second(step, carry):
        peer = peer_of(step)
        copy = second_copy(peer, peer)
        copy.wait_send()
        copy.wait_recv()
        return carry

    lax.fori_loop(0, devices - 1, wait_second, 0)
    stores = [
        pltpu.make_async_copy(landed.at[i], ref, local_sem.at[i])
        for i, ref in enumerate((out_ref, dq_ref, dk_ref, dv_ref))
    ]
    for store in stores:
        store.start()
    for store in stores:
        store.wait()


def fused(seq_count, head_count, queries, key_vectors, value_vectors, out_cotangent, block_mask):
    devices = seq_count * head_count
    rows, width = queries.shape
    tokens, features = rows * devices, width // devices
    kind = queries.dtype
    hbm = pl.BlockSpec(memory_space=pl.ANY)
    one = jax.ShapeDtypeStruct((rows, width), kind)
    return pl.pallas_call(
        functools.partial(fused_kernel, seq_count, head_count),
        out_shape=(one,) * 4,
        in_specs=[pl.BlockSpec(memory_space=pltpu.SMEM)] + [hbm] * 4,
        out_specs=(hbm,) * 4,
        scratch_shapes=[
            pltpu.VMEM((4, rows, width), kind),
            pltpu.VMEM((4, tokens, features), kind),
            pltpu.VMEM((4, tokens, features), kind),
            pltpu.VMEM((4, rows, width), kind),
            pltpu.VMEM((tokens, features), jnp.float32),
            pltpu.VMEM((tokens, features), jnp.float32),
            pltpu.SemaphoreType.DMA((4,)),
            pltpu.SemaphoreType.DMA((devices,)),
            pltpu.SemaphoreType.DMA((devices,)),
            pltpu.SemaphoreType.DMA((devices,)),
            pltpu.SemaphoreType.DMA((devices,)),
        ],
        compiler_params=pltpu.CompilerParams(
            collective_id=0, has_side_effects=True, vmem_limit_bytes=32 * 1024 * 1024
        ),
    )(block_mask, queries, key_vectors, value_vectors, out_cotangent)


def per_device(seq_count, head_count, queries, key_vectors, value_vectors, out_cotangent, block_mask):
    heads = queries.shape[1] // DH
    tokens = queries.shape[0] * seq_count * head_count
    whole_heads = heads % (seq_count * head_count) == 0
    if whole_heads and tokens == block_mask.shape[0] * BLK:
        return fused(
            seq_count, head_count, queries, key_vectors, value_vectors, out_cotangent, block_mask
        )
    return shards(queries, key_vectors, value_vectors, out_cotangent, block_mask)


def solution(mesh):
    placed = (
        P(("seq", "head"), None),
        P(("seq", "head"), None),
        P(("seq", "head"), None),
        P(("seq", "head"), None),
        P(),
    )
    return jax.shard_map(
        functools.partial(per_device, mesh.shape["seq"], mesh.shape["head"]),
        mesh=mesh,
        in_specs=placed,
        out_specs=(
            P(("seq", "head"), None),
            P(("seq", "head"), None),
            P(("seq", "head"), None),
            P(("seq", "head"), None),
        ),
        check_vma=False,
    )
```

```python
import functools

import jax
import jax.numpy as jnp
from jax import lax
from jax.experimental import pallas as pl
from jax.experimental.pallas import tpu as pltpu
from jax.sharding import PartitionSpec as P

DH = 128
BLK = 128


NEG = -1e30


def from_behind(block, axis, distance):
    devices = range(lax.axis_size(axis))
    route = [(i - distance, i) for i in devices if i - distance in devices]
    return lax.ppermute(block, axis, route)


def pick_block(offset, blocks, own, arrived):
    if offset == 0:
        return own
    if offset <= blocks:
        joined = jnp.concatenate([arrived[1], own], axis=0)
        return joined[blocks - offset : 2 * blocks - offset]
    return arrived[offset // blocks]


def shards(queries, key_vectors, value_vectors, out_cotangent, block_mask):
    seq_count = lax.axis_size("seq")
    seq_index = lax.axis_index("seq")
    head_queries, head_keys, head_values, head_grads = (
        lax.all_to_all(queries, "head", split_axis=1, concat_axis=0, tiled=True),
        lax.all_to_all(key_vectors, "head", split_axis=1, concat_axis=0, tiled=True),
        lax.all_to_all(value_vectors, "head", split_axis=1, concat_axis=0, tiled=True),
        lax.all_to_all(out_cotangent, "head", split_axis=1, concat_axis=0, tiled=True),
    )
    patches = head_queries.shape[0]
    local_heads = head_queries.shape[1] // DH
    blocks = patches // BLK
    block_shape = (blocks, BLK, local_heads, DH)
    query_own = head_queries.reshape(block_shape)
    key_own = head_keys.reshape(block_shape)
    value_own = head_values.reshape(block_shape)
    grad_own = head_grads.reshape(block_shape)
    columns = block_mask.shape[1]
    offsets = [0] + [2**level for level in range(columns - 1)]
    distances = [2**level for level in range(seq_count.bit_length() - 1)]
    score_scale = DH ** (-0.5)
    my_mask = lax.dynamic_slice_in_dim(block_mask, seq_index * blocks, blocks, 0)
    arrived_keys = {}
    arrived_values = {}
    for distance in distances:
        moved = from_behind((key_own, value_own), "seq", distance)
        arrived_keys[distance] = moved[0]
        arrived_values[distance] = moved[1]
    keys_all = jnp.stack([pick_block(offset, blocks, key_own, arrived_keys) for offset in offsets])
    values_all = jnp.stack(
        [pick_block(offset, blocks, value_own, arrived_values) for offset in offsets]
    )
    position = jnp.arange(BLK)
    causal = position[None, :] <= position[:, None]
    later = jnp.arange(columns)[None, :, None] > 0
    allowed = (my_mask[:, None, None, :, None] == 1) & (
        later[None, None] | causal[None, None, :, None, :]
    )
    scores = (
        jnp.einsum("bqhd,jbkhd->bhqjk", query_own, keys_all, preferred_element_type=jnp.float32)
        * score_scale
    )
    scores = jnp.where(allowed, scores, NEG)
    row_max = jnp.max(scores, axis=(3, 4))
    row_total = jnp.sum(jnp.exp(scores - row_max[..., None, None]), axis=(3, 4))
    log_total = row_max + jnp.log(row_total)
    weights = jnp.exp(scores - log_total[..., None, None])
    rounded = weights.astype(jnp.bfloat16)
    attended = jnp.einsum(
        "bhqjk,jbkhd->bqhd", rounded, values_all, preferred_element_type=jnp.float32
    ).astype(jnp.bfloat16)
    attended_out = lax.all_to_all(
        attended.reshape(patches, local_heads * DH), "head", split_axis=0, concat_axis=1, tiled=True
    )
    row_delta = jnp.einsum("bqhd,bqhd->bhq", grad_own, attended, preferred_element_type=jnp.float32)
    grad_weights = jnp.einsum(
        "bqhd,jbkhd->bhqjk", grad_own, values_all, preferred_element_type=jnp.float32
    )
    grad_scores = (weights * (grad_weights - row_delta[..., None, None]) * score_scale).astype(
        jnp.bfloat16
    )
    query_grad = jnp.einsum(
        "bhqjk,jbkhd->bqhd", grad_scores, keys_all, preferred_element_type=jnp.float32
    ).astype(jnp.bfloat16)
    key_parts = jnp.einsum(
        "bhqjk,bqhd->jbkhd", grad_scores, query_own, preferred_element_type=jnp.float32
    )
    value_parts = jnp.einsum(
        "bhqjk,bqhd->jbkhd", rounded, grad_own, preferred_element_type=jnp.float32
    )
    key_grad = key_parts[0]
    value_grad = value_parts[0]
    near_keys = jnp.zeros((2 * blocks,) + block_shape[1:], jnp.float32)
    near_values = jnp.zeros((2 * blocks,) + block_shape[1:], jnp.float32)
    outgoing_keys = {}
    outgoing_values = {}
    for column in range(1, columns):
        offset = offsets[column]
        if offset <= blocks:
            padding = ((blocks - offset, offset), (0, 0), (0, 0), (0, 0))
            near_keys = jnp.pad(key_parts[column], padding)
            near_values = jnp.pad(value_parts[column], padding)
        else:
            outgoing_keys[offset // blocks] = key_parts[column]
            outgoing_values[offset // blocks] = value_parts[column]
    key_grad = key_grad + near_keys[blocks:]
    value_grad = value_grad + near_values[blocks:]
    outgoing_keys[1] = near_keys[:blocks]
    outgoing_values[1] = near_values[:blocks]
    for distance in distances:
        returned = (
            from_behind(outgoing_keys[distance].astype(jnp.bfloat16), "seq", -distance).astype(
                jnp.float32
            ),
            from_behind(outgoing_values[distance].astype(jnp.bfloat16), "seq", -distance).astype(
                jnp.float32
            ),
        )
        key_grad = key_grad + returned[0]
        value_grad = value_grad + returned[1]
    flat = (patches, local_heads * DH)
    grads_out = (
        lax.all_to_all(query_grad.reshape(flat), "head", split_axis=0, concat_axis=1, tiled=True),
        lax.all_to_all(
            key_grad.astype(jnp.bfloat16).reshape(flat),
            "head",
            split_axis=0,
            concat_axis=1,
            tiled=True,
        ),
        lax.all_to_all(
            value_grad.astype(jnp.bfloat16).reshape(flat),
            "head",
            split_axis=0,
            concat_axis=1,
            tiled=True,
        ),
    )
    return (attended_out, grads_out[0], grads_out[1], grads_out[2])


def rows_of(index, size):
    return pl.ds(pl.multiple_of(index * size, size), size)


def fused_kernel(
    seq_count,
    head_count,
    mask_ref,
    q_ref,
    k_ref,
    v_ref,
    g_ref,
    landed,
    outbound,
    inbound,
    results,
    key_sum,
    value_sum,
    local_sem,
    send_one,
    recv_one,
    send_two,
    recv_two,
):
    devices = seq_count * head_count
    rows, width = q_ref.shape
    features = width // devices
    local_heads = features // DH
    columns, blocks = mask_ref.shape
    offsets = [0] + [2**level for level in range(columns - 1)]
    scale = DH ** (-0.5)
    me = lax.axis_index("seq") * head_count + lax.axis_index("head")

    def place(index):
        return (index // head_count, index % head_count)

    loads = [
        pltpu.make_async_copy(ref, outbound.at[i], local_sem.at[i])
        for i, ref in enumerate((q_ref, k_ref, v_ref, g_ref))
    ]
    for load in loads:
        load.start()

    barrier = pltpu.get_barrier_semaphore()

    def greet(step, carry):
        pl.semaphore_signal(
            barrier,
            inc=1,
            device_id=place((me + step) % devices),
            device_id_type=pl.DeviceIdType.MESH,
        )
        return carry

    lax.fori_loop(1, devices, greet, 0)
    for load in loads:
        load.wait()
    pl.semaphore_wait(barrier, devices - 1)

    def peer_of(step):
        turn = devices // 2 + (1 - 2 * (step % 2)) * ((step + 1) // 2)
        return (me + turn) % devices

    def first_copy(peer, slot):
        return pltpu.make_async_remote_copy(
            src_ref=outbound.at[:, :, rows_of(peer, features)],
            dst_ref=inbound.at[:, rows_of(slot, rows), :],
            send_sem=send_one.at[peer],
            recv_sem=recv_one.at[slot],
            device_id=place(peer),
            device_id_type=pl.DeviceIdType.MESH,
        )

    def second_copy(peer, slot):
        return pltpu.make_async_remote_copy(
            src_ref=results.at[:, rows_of(peer, rows), :],
            dst_ref=landed.at[:, :, rows_of(slot, features)],
            send_sem=send_two.at[peer],
            recv_sem=recv_two.at[slot],
            device_id=place(peer),
            device_id_type=pl.DeviceIdType.MESH,
        )

    def start_first(step, carry):
        first_copy(peer_of(step), me).start()
        return carry

    lax.fori_loop(0, devices - 1, start_first, 0)
    inbound[:, rows_of(me, rows), :] = outbound[:, :, rows_of(me, features)]

    def wait_first(step, carry):
        peer = peer_of(step)
        copy = first_copy(peer, peer)
        copy.wait_send()
        copy.wait_recv()
        return carry

    lax.fori_loop(0, devices - 1, wait_first, 0)

    query_at = lax.broadcasted_iota(jnp.int32, (BLK, BLK), 0)
    key_at = lax.broadcasted_iota(jnp.int32, (BLK, BLK), 1)
    causal = key_at <= query_at

    def dot(a, b, dims):
        return lax.dot_general(a, b, (dims, ((), ())), preferred_element_type=jnp.float32)

    def attend(block, carry):
        here = rows_of(block, BLK)
        sources = [rows_of(jnp.maximum(block - offset, 0), BLK) for offset in offsets]
        for head in range(local_heads):
            part = slice(head * DH, (head + 1) * DH)
            query = inbound[0, here, part]
            grad = inbound[3, here, part]
            keys = jnp.concatenate([inbound[1, source, part] for source in sources], axis=0)
            values = jnp.concatenate([inbound[2, source, part] for source in sources], axis=0)
            scores = dot(query, keys, ((1,), (1,))) * scale
            pieces = []
            for j in range(columns):
                live = mask_ref[j, block] == 1
                piece = scores[:, j * BLK : (j + 1) * BLK]
                if j == 0:
                    piece = jnp.where(causal, piece, NEG)
                pieces.append(jnp.where(live, piece, NEG))
            scores = jnp.concatenate(pieces, axis=1)
            row_max = jnp.max(scores, axis=1, keepdims=True)
            raised = jnp.exp(scores - row_max)
            total = jnp.sum(raised, axis=1, keepdims=True)
            weights = raised * (1.0 / total)
            rounded = weights.astype(jnp.bfloat16)
            attended = dot(rounded, values, ((1,), (0,))).astype(jnp.bfloat16)
            delta = jnp.sum(
                grad.astype(jnp.float32) * attended.astype(jnp.float32), axis=1, keepdims=True
            )
            grad_weights = dot(grad, values, ((1,), (1,)))
            grad_scores = (weights * (grad_weights - delta) * scale).astype(jnp.bfloat16)
            query_grad = dot(grad_scores, keys, ((1,), (0,))).astype(jnp.bfloat16)
            key_parts = dot(grad_scores, query, ((0,), (0,)))
            value_parts = dot(rounded, grad, ((0,), (0,)))
            results[0, here, part] = attended
            results[1, here, part] = query_grad
            key_sum[here, part] = key_parts[:BLK]
            value_sum[here, part] = value_parts[:BLK]
            for j in range(1, columns):
                piece = slice(j * BLK, (j + 1) * BLK)
                key_sum[sources[j], part] += key_parts[piece]
                value_sum[sources[j], part] += value_parts[piece]
        return carry

    lax.fori_loop(0, blocks, attend, 0)

    def finish(block, carry):
        here = rows_of(block, BLK)
        results[2, here, :] = key_sum[here, :].astype(jnp.bfloat16)
        results[3, here, :] = value_sum[here, :].astype(jnp.bfloat16)
        return carry

    lax.fori_loop(0, blocks, finish, 0)

    def start_second(step, carry):
        second_copy(peer_of(step), me).start()
        return carry

    lax.fori_loop(0, devices - 1, start_second, 0)
    own = pltpu.make_async_copy(
        results.at[:, rows_of(me, rows), :],
        landed.at[:, :, rows_of(me, features)],
        local_sem.at[0],
    )
    own.start()

    def wait_second(step, carry):
        peer = peer_of(step)
        copy = second_copy(peer, peer)
        copy.wait_send()
        copy.wait_recv()
        return carry

    lax.fori_loop(0, devices - 1, wait_second, 0)
    own.wait()


def hand_out(landed, out_ref, dq_ref, dk_ref, dv_ref, sem):
    stores = [
        pltpu.make_async_copy(landed.at[i], ref, sem.at[i])
        for i, ref in enumerate((out_ref, dq_ref, dk_ref, dv_ref))
    ]
    for store in stores:
        store.start()
    for store in stores:
        store.wait()


def fused(seq_count, head_count, queries, key_vectors, value_vectors, out_cotangent, block_mask):
    devices = seq_count * head_count
    rows, width = queries.shape
    tokens, features = rows * devices, width // devices
    kind = queries.dtype
    hbm = pl.BlockSpec(memory_space=pltpu.HBM)
    anywhere = pl.BlockSpec(memory_space=pl.ANY)
    one = jax.ShapeDtypeStruct((rows, width), kind)
    landed = pl.pallas_call(
        functools.partial(fused_kernel, seq_count, head_count),
        out_shape=jax.ShapeDtypeStruct((4, rows, width), kind),
        in_specs=[pl.BlockSpec(memory_space=pltpu.SMEM)] + [hbm] * 4,
        out_specs=anywhere,
        scratch_shapes=[
            pltpu.VMEM((4, rows, width), kind),
            pltpu.VMEM((4, tokens, features), kind),
            pltpu.VMEM((4, tokens, features), kind),
            pltpu.VMEM((tokens, features), jnp.float32),
            pltpu.VMEM((tokens, features), jnp.float32),
            pltpu.SemaphoreType.DMA((4,)),
            pltpu.SemaphoreType.DMA((devices,)),
            pltpu.SemaphoreType.DMA((devices,)),
            pltpu.SemaphoreType.DMA((devices,)),
            pltpu.SemaphoreType.DMA((devices,)),
        ],
        compiler_params=pltpu.CompilerParams(
            collective_id=0, has_side_effects=True, vmem_limit_bytes=62 * 1024 * 1024
        ),
    )(block_mask.T, queries, key_vectors, value_vectors, out_cotangent)
    return pl.pallas_call(
        hand_out,
        out_shape=(one,) * 4,
        in_specs=[pl.BlockSpec(memory_space=pltpu.VMEM)],
        out_specs=(hbm,) * 4,
        scratch_shapes=[pltpu.SemaphoreType.DMA((4,))],
    )(landed)


def per_device(seq_count, head_count, queries, key_vectors, value_vectors, out_cotangent, block_mask):
    heads = queries.shape[1] // DH
    tokens = queries.shape[0] * seq_count * head_count
    whole_heads = heads % (seq_count * head_count) == 0
    if whole_heads and tokens == block_mask.shape[0] * BLK:
        return fused(
            seq_count, head_count, queries, key_vectors, value_vectors, out_cotangent, block_mask
        )
    return shards(queries, key_vectors, value_vectors, out_cotangent, block_mask)


def solution(mesh):
    placed = (
        P(("seq", "head"), None),
        P(("seq", "head"), None),
        P(("seq", "head"), None),
        P(("seq", "head"), None),
        P(),
    )
    return jax.shard_map(
        functools.partial(per_device, mesh.shape["seq"], mesh.shape["head"]),
        mesh=mesh,
        in_specs=placed,
        out_specs=(
            P(("seq", "head"), None),
            P(("seq", "head"), None),
            P(("seq", "head"), None),
            P(("seq", "head"), None),
        ),
        check_vma=False,
    )
```

```python
import functools

import jax
import jax.numpy as jnp
from jax import lax
from jax.experimental import pallas as pl
from jax.experimental.pallas import tpu as pltpu
from jax.sharding import PartitionSpec as P

DH = 128
BLK = 128


NEG = -1e30


def from_behind(block, axis, distance):
    devices = range(lax.axis_size(axis))
    route = [(i - distance, i) for i in devices if i - distance in devices]
    return lax.ppermute(block, axis, route)


def pick_block(offset, blocks, own, arrived):
    if offset == 0:
        return own
    if offset <= blocks:
        joined = jnp.concatenate([arrived[1], own], axis=0)
        return joined[blocks - offset : 2 * blocks - offset]
    return arrived[offset // blocks]


def shards(queries, key_vectors, value_vectors, out_cotangent, block_mask):
    seq_count = lax.axis_size("seq")
    seq_index = lax.axis_index("seq")
    head_queries, head_keys, head_values, head_grads = (
        lax.all_to_all(queries, "head", split_axis=1, concat_axis=0, tiled=True),
        lax.all_to_all(key_vectors, "head", split_axis=1, concat_axis=0, tiled=True),
        lax.all_to_all(value_vectors, "head", split_axis=1, concat_axis=0, tiled=True),
        lax.all_to_all(out_cotangent, "head", split_axis=1, concat_axis=0, tiled=True),
    )
    patches = head_queries.shape[0]
    local_heads = head_queries.shape[1] // DH
    blocks = patches // BLK
    block_shape = (blocks, BLK, local_heads, DH)
    query_own = head_queries.reshape(block_shape)
    key_own = head_keys.reshape(block_shape)
    value_own = head_values.reshape(block_shape)
    grad_own = head_grads.reshape(block_shape)
    columns = block_mask.shape[1]
    offsets = [0] + [2**level for level in range(columns - 1)]
    distances = [2**level for level in range(seq_count.bit_length() - 1)]
    score_scale = DH ** (-0.5)
    my_mask = lax.dynamic_slice_in_dim(block_mask, seq_index * blocks, blocks, 0)
    arrived_keys = {}
    arrived_values = {}
    for distance in distances:
        moved = from_behind((key_own, value_own), "seq", distance)
        arrived_keys[distance] = moved[0]
        arrived_values[distance] = moved[1]
    keys_all = jnp.stack([pick_block(offset, blocks, key_own, arrived_keys) for offset in offsets])
    values_all = jnp.stack(
        [pick_block(offset, blocks, value_own, arrived_values) for offset in offsets]
    )
    position = jnp.arange(BLK)
    causal = position[None, :] <= position[:, None]
    later = jnp.arange(columns)[None, :, None] > 0
    allowed = (my_mask[:, None, None, :, None] == 1) & (
        later[None, None] | causal[None, None, :, None, :]
    )
    scores = (
        jnp.einsum("bqhd,jbkhd->bhqjk", query_own, keys_all, preferred_element_type=jnp.float32)
        * score_scale
    )
    scores = jnp.where(allowed, scores, NEG)
    row_max = jnp.max(scores, axis=(3, 4))
    row_total = jnp.sum(jnp.exp(scores - row_max[..., None, None]), axis=(3, 4))
    log_total = row_max + jnp.log(row_total)
    weights = jnp.exp(scores - log_total[..., None, None])
    rounded = weights.astype(jnp.bfloat16)
    attended = jnp.einsum(
        "bhqjk,jbkhd->bqhd", rounded, values_all, preferred_element_type=jnp.float32
    ).astype(jnp.bfloat16)
    attended_out = lax.all_to_all(
        attended.reshape(patches, local_heads * DH), "head", split_axis=0, concat_axis=1, tiled=True
    )
    row_delta = jnp.einsum("bqhd,bqhd->bhq", grad_own, attended, preferred_element_type=jnp.float32)
    grad_weights = jnp.einsum(
        "bqhd,jbkhd->bhqjk", grad_own, values_all, preferred_element_type=jnp.float32
    )
    grad_scores = (weights * (grad_weights - row_delta[..., None, None]) * score_scale).astype(
        jnp.bfloat16
    )
    query_grad = jnp.einsum(
        "bhqjk,jbkhd->bqhd", grad_scores, keys_all, preferred_element_type=jnp.float32
    ).astype(jnp.bfloat16)
    key_parts = jnp.einsum(
        "bhqjk,bqhd->jbkhd", grad_scores, query_own, preferred_element_type=jnp.float32
    )
    value_parts = jnp.einsum(
        "bhqjk,bqhd->jbkhd", rounded, grad_own, preferred_element_type=jnp.float32
    )
    key_grad = key_parts[0]
    value_grad = value_parts[0]
    near_keys = jnp.zeros((2 * blocks,) + block_shape[1:], jnp.float32)
    near_values = jnp.zeros((2 * blocks,) + block_shape[1:], jnp.float32)
    outgoing_keys = {}
    outgoing_values = {}
    for column in range(1, columns):
        offset = offsets[column]
        if offset <= blocks:
            padding = ((blocks - offset, offset), (0, 0), (0, 0), (0, 0))
            near_keys = jnp.pad(key_parts[column], padding)
            near_values = jnp.pad(value_parts[column], padding)
        else:
            outgoing_keys[offset // blocks] = key_parts[column]
            outgoing_values[offset // blocks] = value_parts[column]
    key_grad = key_grad + near_keys[blocks:]
    value_grad = value_grad + near_values[blocks:]
    outgoing_keys[1] = near_keys[:blocks]
    outgoing_values[1] = near_values[:blocks]
    for distance in distances:
        returned = (
            from_behind(outgoing_keys[distance].astype(jnp.bfloat16), "seq", -distance).astype(
                jnp.float32
            ),
            from_behind(outgoing_values[distance].astype(jnp.bfloat16), "seq", -distance).astype(
                jnp.float32
            ),
        )
        key_grad = key_grad + returned[0]
        value_grad = value_grad + returned[1]
    flat = (patches, local_heads * DH)
    grads_out = (
        lax.all_to_all(query_grad.reshape(flat), "head", split_axis=0, concat_axis=1, tiled=True),
        lax.all_to_all(
            key_grad.astype(jnp.bfloat16).reshape(flat),
            "head",
            split_axis=0,
            concat_axis=1,
            tiled=True,
        ),
        lax.all_to_all(
            value_grad.astype(jnp.bfloat16).reshape(flat),
            "head",
            split_axis=0,
            concat_axis=1,
            tiled=True,
        ),
    )
    return (attended_out, grads_out[0], grads_out[1], grads_out[2])


def rows_of(index, size):
    return pl.ds(pl.multiple_of(index * size, size), size)


def fused_kernel(
    seq_count,
    head_count,
    mask_ref,
    q_ref,
    k_ref,
    v_ref,
    g_ref,
    landed,
    returned,
    outbound,
    inbound,
    results,
    results_back,
    key_sum,
    value_sum,
    local_sem,
    own_in_sem,
    own_out_sem,
    send_in,
    recv_in,
    send_out,
    recv_out,
):
    devices = seq_count * head_count
    half = devices // 2
    rows, width = q_ref.shape
    local_heads = width // DH // half
    columns, blocks = mask_ref.shape
    half_blocks = blocks // 2
    half_rows = half * rows
    offsets = [0] + [2**level for level in range(columns - 1)]
    scale = DH ** (-0.5)
    me = lax.axis_index("seq") * head_count + lax.axis_index("head")
    upper = me // half
    spot = me % half

    def place(index):
        return (index // head_count, index % head_count)

    loads = [
        pltpu.make_async_copy(ref, outbound.at[i], local_sem.at[i])
        for i, ref in enumerate((k_ref, v_ref, q_ref, g_ref))
    ]
    for load in loads:
        load.start()

    barrier = pltpu.get_barrier_semaphore()

    def greet(step, carry):
        pl.semaphore_signal(
            barrier,
            inc=1,
            device_id=place((me + step) % devices),
            device_id_type=pl.DeviceIdType.MESH,
        )
        return carry

    lax.fori_loop(1, devices, greet, 0)

    @pl.when(upper == 0)
    def clear():
        inbound[:, 0:2, 0:half_rows, :] = jnp.zeros(
            (local_heads, 2, half_rows, DH), inbound.dtype
        )

    for load in loads:
        load.wait()
    pl.semaphore_wait(barrier, devices - 1)

    def near(step):
        turn = half // 2 + (1 - 2 * (step % 2)) * ((step + 1) // 2)
        return upper * half + (spot + turn) % half

    def across(step):
        return (1 - upper) * half + (spot + step) % half

    def copy_in(head, peer, source):
        return pltpu.make_async_remote_copy(
            src_ref=outbound.at[:, :, rows_of((peer % half) * local_heads + head, DH)],
            dst_ref=inbound.at[head, :, rows_of(half + source % half, rows), :],
            send_sem=send_in.at[head, peer],
            recv_sem=recv_in.at[head, source],
            device_id=place(peer),
            device_id_type=pl.DeviceIdType.MESH,
        )

    def copy_up(head, peer, source):
        return pltpu.make_async_remote_copy(
            src_ref=outbound.at[0:2, :, rows_of((peer % half) * local_heads + head, DH)],
            dst_ref=inbound.at[head, 0:2, rows_of(source % half, rows), :],
            send_sem=send_in.at[head, peer],
            recv_sem=recv_in.at[head, source],
            device_id=place(peer),
            device_id_type=pl.DeviceIdType.MESH,
        )

    def copy_out(head, peer, source):
        return pltpu.make_async_remote_copy(
            src_ref=results.at[head, :, rows_of(peer % half, rows), :],
            dst_ref=landed.at[:, :, rows_of((source % half) * local_heads + head, DH)],
            send_sem=send_out.at[head, peer],
            recv_sem=recv_out.at[head, source],
            device_id=place(peer),
            device_id_type=pl.DeviceIdType.MESH,
        )

    def copy_back(head, peer, source):
        return pltpu.make_async_remote_copy(
            src_ref=results_back.at[head, :, rows_of(peer % half, rows), :],
            dst_ref=returned.at[:, :, rows_of((source % half) * local_heads + head, DH)],
            send_sem=send_out.at[head, peer],
            recv_sem=recv_out.at[head, source],
            device_id=place(peer),
            device_id_type=pl.DeviceIdType.MESH,
        )

    def own_in(head):
        return pltpu.make_async_copy(
            outbound.at[:, :, rows_of(spot * local_heads + head, DH)],
            inbound.at[head, :, rows_of(half + spot, rows), :],
            own_in_sem.at[head],
        )

    def own_out(head):
        return pltpu.make_async_copy(
            results.at[head, :, rows_of(spot, rows), :],
            landed.at[:, :, rows_of(spot * local_heads + head, DH)],
            own_out_sem.at[head],
        )

    def each(count, act):
        def step_of(step, carry):
            act(step)
            return carry

        lax.fori_loop(0, count, step_of, 0)

    for head in range(local_heads):

        @pl.when(upper == 0)
        def send_up():
            each(half, lambda step: copy_up(head, across(step), me).start())

        each(half - 1, lambda step: copy_in(head, near(step), me).start())
        own_in(head).start()

    query_at = lax.broadcasted_iota(jnp.int32, (BLK, BLK), 0)
    key_at = lax.broadcasted_iota(jnp.int32, (BLK, BLK), 1)
    causal = key_at <= query_at

    def dot(a, b, dims):
        return lax.dot_general(a, b, (dims, ((), ())), preferred_element_type=jnp.float32)

    def attend(head, block):
        here = rows_of(block, BLK)
        own = rows_of(half_blocks + block, BLK)
        sources = [rows_of(half_blocks + block - offset, BLK) for offset in offsets]
        query = inbound[head, 2, own, :]
        grad = inbound[head, 3, own, :]
        keys = jnp.concatenate([inbound[head, 0, source, :] for source in sources], axis=0)
        values = jnp.concatenate([inbound[head, 1, source, :] for source in sources], axis=0)
        scores = dot(query, keys, ((1,), (1,))) * scale
        pieces = []
        for j in range(columns):
            live = mask_ref[j, upper * half_blocks + block] == 1
            piece = scores[:, j * BLK : (j + 1) * BLK]
            if j == 0:
                piece = jnp.where(causal, piece, NEG)
            pieces.append(jnp.where(live, piece, NEG))
        scores = jnp.concatenate(pieces, axis=1)
        row_max = jnp.max(scores, axis=1, keepdims=True)
        raised = jnp.exp(scores - row_max)
        total = jnp.sum(raised, axis=1, keepdims=True)
        weights = raised * (1.0 / total)
        rounded = weights.astype(jnp.bfloat16)
        attended = dot(rounded, values, ((1,), (0,))).astype(jnp.bfloat16)
        delta = jnp.sum(
            grad.astype(jnp.float32) * attended.astype(jnp.float32), axis=1, keepdims=True
        )
        grad_weights = dot(grad, values, ((1,), (1,)))
        grad_scores = (weights * (grad_weights - delta) * scale).astype(jnp.bfloat16)
        query_grad = dot(grad_scores, keys, ((1,), (0,))).astype(jnp.bfloat16)
        key_parts = dot(grad_scores, query, ((0,), (0,)))
        value_parts = dot(rounded, grad, ((0,), (0,)))
        results[head, 0, here, :] = attended
        results[head, 1, here, :] = query_grad
        key_sum[own, :] = key_parts[:BLK]
        value_sum[own, :] = value_parts[:BLK]
        for j in range(1, columns):
            piece = slice(j * BLK, (j + 1) * BLK)
            key_sum[sources[j], :] += key_parts[piece]
            value_sum[sources[j], :] += value_parts[piece]

    for head in range(local_heads):
        key_sum[0:half_rows, :] = jnp.zeros((half_rows, DH), jnp.float32)
        value_sum[0:half_rows, :] = jnp.zeros((half_rows, DH), jnp.float32)
        own_in(head).wait()
        each(half - 1, lambda step: copy_in(head, near(step), near(step)).wait_recv())

        @pl.when(upper == 1)
        def await_lower():
            each(half, lambda step: copy_up(head, across(step), across(step)).wait_recv())

        each(half_blocks, functools.partial(attend, head))

        @pl.when(upper == 1)
        def send_back():
            results_back[head, 0] = key_sum[0:half_rows, :].astype(jnp.bfloat16)
            results_back[head, 1] = value_sum[0:half_rows, :].astype(jnp.bfloat16)
            each(half, lambda step: copy_back(head, across(step), me).start())

        results[head, 2] = key_sum[half_rows : 2 * half_rows, :].astype(jnp.bfloat16)
        results[head, 3] = value_sum[half_rows : 2 * half_rows, :].astype(jnp.bfloat16)
        each(half - 1, lambda step: copy_out(head, near(step), me).start())
        own_out(head).start()

    for head in range(local_heads):
        own_out(head).wait()

        def settle(step):
            peer = near(step)
            copy_in(head, peer, peer).wait_send()
            copy = copy_out(head, peer, peer)
            copy.wait_send()
            copy.wait_recv()

        each(half - 1, settle)

        @pl.when(upper == 0)
        def settle_lower():
            def one(step):
                peer = across(step)
                copy_up(head, peer, peer).wait_send()
                copy_back(head, peer, peer).wait_recv()

            each(half, one)

        @pl.when(upper == 1)
        def settle_upper():
            each(half, lambda step: copy_back(head, across(step), across(step)).wait_send())


def hand_out(seq_count, landed, returned, out_ref, dq_ref, dk_ref, dv_ref):
    lower = lax.axis_index("seq") < seq_count // 2
    out_ref[...] = landed[0]
    dq_ref[...] = landed[1]
    for i, ref in enumerate((dk_ref, dv_ref)):
        own = landed[2 + i]
        both = own.astype(jnp.float32) + returned[i].astype(jnp.float32)
        ref[...] = jnp.where(lower, both.astype(own.dtype), own)


def fused(seq_count, head_count, queries, key_vectors, value_vectors, out_cotangent, block_mask):
    devices = seq_count * head_count
    half = devices // 2
    rows, width = queries.shape
    tokens, local_heads = rows * devices, width // DH // half
    kind = queries.dtype
    anywhere = pl.BlockSpec(memory_space=pl.ANY)
    vmem = pl.BlockSpec(memory_space=pltpu.VMEM)
    one = jax.ShapeDtypeStruct((rows, width), kind)
    landed, returned = pl.pallas_call(
        functools.partial(fused_kernel, seq_count, head_count),
        out_shape=(
            jax.ShapeDtypeStruct((4, rows, width), kind),
            jax.ShapeDtypeStruct((2, rows, width), kind),
        ),
        in_specs=[pl.BlockSpec(memory_space=pltpu.SMEM)] + [anywhere] * 4,
        out_specs=(anywhere,) * 2,
        scratch_shapes=[
            pltpu.VMEM((4, rows, width), kind),
            pltpu.VMEM((local_heads, 4, tokens, DH), kind),
            pltpu.VMEM((local_heads, 4, tokens // 2, DH), kind),
            pltpu.VMEM((local_heads, 2, tokens // 2, DH), kind),
            pltpu.VMEM((tokens, DH), jnp.float32),
            pltpu.VMEM((tokens, DH), jnp.float32),
            pltpu.SemaphoreType.DMA((4,)),
            pltpu.SemaphoreType.DMA((local_heads,)),
            pltpu.SemaphoreType.DMA((local_heads,)),
            pltpu.SemaphoreType.DMA((local_heads, devices)),
            pltpu.SemaphoreType.DMA((local_heads, devices)),
            pltpu.SemaphoreType.DMA((local_heads, devices)),
            pltpu.SemaphoreType.DMA((local_heads, devices)),
        ],
        compiler_params=pltpu.CompilerParams(
            collective_id=0, has_side_effects=True, vmem_limit_bytes=62 * 1024 * 1024
        ),
    )(block_mask.T, queries, key_vectors, value_vectors, out_cotangent)
    return pl.pallas_call(
        functools.partial(hand_out, seq_count),
        out_shape=(one,) * 4,
        in_specs=[vmem] * 2,
        out_specs=(vmem,) * 4,
    )(landed, returned)


def per_device(seq_count, head_count, queries, key_vectors, value_vectors, out_cotangent, block_mask):
    heads = queries.shape[1] // DH
    devices = seq_count * head_count
    tokens = queries.shape[0] * devices
    blocks, columns = block_mask.shape
    halves = seq_count % 2 == 0 and blocks % 2 == 0 and tokens == blocks * BLK
    if halves and heads % (devices // 2) == 0 and 2 ** max(columns - 2, 0) <= blocks // 2:
        return fused(
            seq_count, head_count, queries, key_vectors, value_vectors, out_cotangent, block_mask
        )
    return shards(queries, key_vectors, value_vectors, out_cotangent, block_mask)


def solution(mesh):
    placed = (
        P(("seq", "head"), None),
        P(("seq", "head"), None),
        P(("seq", "head"), None),
        P(("seq", "head"), None),
        P(),
    )
    return jax.shard_map(
        functools.partial(per_device, mesh.shape["seq"], mesh.shape["head"]),
        mesh=mesh,
        in_specs=placed,
        out_specs=(
            P(("seq", "head"), None),
            P(("seq", "head"), None),
            P(("seq", "head"), None),
            P(("seq", "head"), None),
        ),
        check_vma=False,
    )
```

```python
import functools

import jax
import jax.numpy as jnp
from jax import lax
from jax.experimental import pallas as pl
from jax.experimental.pallas import tpu as pltpu
from jax.sharding import PartitionSpec as P

DH = 128
BLK = 128


NEG = -1e30


def from_behind(block, axis, distance):
    devices = range(lax.axis_size(axis))
    route = [(i - distance, i) for i in devices if i - distance in devices]
    return lax.ppermute(block, axis, route)


def pick_block(offset, blocks, own, arrived):
    if offset == 0:
        return own
    if offset <= blocks:
        joined = jnp.concatenate([arrived[1], own], axis=0)
        return joined[blocks - offset : 2 * blocks - offset]
    return arrived[offset // blocks]


def shards(queries, key_vectors, value_vectors, out_cotangent, block_mask):
    seq_count = lax.axis_size("seq")
    seq_index = lax.axis_index("seq")
    head_queries, head_keys, head_values, head_grads = (
        lax.all_to_all(queries, "head", split_axis=1, concat_axis=0, tiled=True),
        lax.all_to_all(key_vectors, "head", split_axis=1, concat_axis=0, tiled=True),
        lax.all_to_all(value_vectors, "head", split_axis=1, concat_axis=0, tiled=True),
        lax.all_to_all(out_cotangent, "head", split_axis=1, concat_axis=0, tiled=True),
    )
    patches = head_queries.shape[0]
    local_heads = head_queries.shape[1] // DH
    blocks = patches // BLK
    block_shape = (blocks, BLK, local_heads, DH)
    query_own = head_queries.reshape(block_shape)
    key_own = head_keys.reshape(block_shape)
    value_own = head_values.reshape(block_shape)
    grad_own = head_grads.reshape(block_shape)
    columns = block_mask.shape[1]
    offsets = [0] + [2**level for level in range(columns - 1)]
    distances = [2**level for level in range(seq_count.bit_length() - 1)]
    score_scale = DH ** (-0.5)
    my_mask = lax.dynamic_slice_in_dim(block_mask, seq_index * blocks, blocks, 0)
    arrived_keys = {}
    arrived_values = {}
    for distance in distances:
        moved = from_behind((key_own, value_own), "seq", distance)
        arrived_keys[distance] = moved[0]
        arrived_values[distance] = moved[1]
    keys_all = jnp.stack([pick_block(offset, blocks, key_own, arrived_keys) for offset in offsets])
    values_all = jnp.stack(
        [pick_block(offset, blocks, value_own, arrived_values) for offset in offsets]
    )
    position = jnp.arange(BLK)
    causal = position[None, :] <= position[:, None]
    later = jnp.arange(columns)[None, :, None] > 0
    allowed = (my_mask[:, None, None, :, None] == 1) & (
        later[None, None] | causal[None, None, :, None, :]
    )
    scores = (
        jnp.einsum("bqhd,jbkhd->bhqjk", query_own, keys_all, preferred_element_type=jnp.float32)
        * score_scale
    )
    scores = jnp.where(allowed, scores, NEG)
    row_max = jnp.max(scores, axis=(3, 4))
    row_total = jnp.sum(jnp.exp(scores - row_max[..., None, None]), axis=(3, 4))
    log_total = row_max + jnp.log(row_total)
    weights = jnp.exp(scores - log_total[..., None, None])
    rounded = weights.astype(jnp.bfloat16)
    attended = jnp.einsum(
        "bhqjk,jbkhd->bqhd", rounded, values_all, preferred_element_type=jnp.float32
    ).astype(jnp.bfloat16)
    attended_out = lax.all_to_all(
        attended.reshape(patches, local_heads * DH), "head", split_axis=0, concat_axis=1, tiled=True
    )
    row_delta = jnp.einsum("bqhd,bqhd->bhq", grad_own, attended, preferred_element_type=jnp.float32)
    grad_weights = jnp.einsum(
        "bqhd,jbkhd->bhqjk", grad_own, values_all, preferred_element_type=jnp.float32
    )
    grad_scores = (weights * (grad_weights - row_delta[..., None, None]) * score_scale).astype(
        jnp.bfloat16
    )
    query_grad = jnp.einsum(
        "bhqjk,jbkhd->bqhd", grad_scores, keys_all, preferred_element_type=jnp.float32
    ).astype(jnp.bfloat16)
    key_parts = jnp.einsum(
        "bhqjk,bqhd->jbkhd", grad_scores, query_own, preferred_element_type=jnp.float32
    )
    value_parts = jnp.einsum(
        "bhqjk,bqhd->jbkhd", rounded, grad_own, preferred_element_type=jnp.float32
    )
    key_grad = key_parts[0]
    value_grad = value_parts[0]
    near_keys = jnp.zeros((2 * blocks,) + block_shape[1:], jnp.float32)
    near_values = jnp.zeros((2 * blocks,) + block_shape[1:], jnp.float32)
    outgoing_keys = {}
    outgoing_values = {}
    for column in range(1, columns):
        offset = offsets[column]
        if offset <= blocks:
            padding = ((blocks - offset, offset), (0, 0), (0, 0), (0, 0))
            near_keys = jnp.pad(key_parts[column], padding)
            near_values = jnp.pad(value_parts[column], padding)
        else:
            outgoing_keys[offset // blocks] = key_parts[column]
            outgoing_values[offset // blocks] = value_parts[column]
    key_grad = key_grad + near_keys[blocks:]
    value_grad = value_grad + near_values[blocks:]
    outgoing_keys[1] = near_keys[:blocks]
    outgoing_values[1] = near_values[:blocks]
    for distance in distances:
        returned = (
            from_behind(outgoing_keys[distance].astype(jnp.bfloat16), "seq", -distance).astype(
                jnp.float32
            ),
            from_behind(outgoing_values[distance].astype(jnp.bfloat16), "seq", -distance).astype(
                jnp.float32
            ),
        )
        key_grad = key_grad + returned[0]
        value_grad = value_grad + returned[1]
    flat = (patches, local_heads * DH)
    grads_out = (
        lax.all_to_all(query_grad.reshape(flat), "head", split_axis=0, concat_axis=1, tiled=True),
        lax.all_to_all(
            key_grad.astype(jnp.bfloat16).reshape(flat),
            "head",
            split_axis=0,
            concat_axis=1,
            tiled=True,
        ),
        lax.all_to_all(
            value_grad.astype(jnp.bfloat16).reshape(flat),
            "head",
            split_axis=0,
            concat_axis=1,
            tiled=True,
        ),
    )
    return (attended_out, grads_out[0], grads_out[1], grads_out[2])


def rows_of(index, size):
    if isinstance(index, int):
        return pl.ds(index * size, size)
    return pl.ds(pl.multiple_of(index * size, size), size)


def fused_kernel(
    seq_count,
    head_count,
    mask_ref,
    q_ref,
    k_ref,
    v_ref,
    g_ref,
    landed,
    returned,
    outbound,
    inbound,
    results,
    results_back,
    key_sum,
    value_sum,
    local_sem,
    own_in_sem,
    own_out_sem,
    send_in,
    recv_in,
    send_out,
    recv_out,
):
    devices = seq_count * head_count
    half = devices // 2
    rows, width = q_ref.shape
    local_heads = width // DH // half
    columns, blocks = mask_ref.shape
    half_blocks = blocks // 2
    half_rows = half * rows
    offsets = [0] + [2**level for level in range(columns - 1)]
    scale = DH ** (-0.5)
    me = lax.axis_index("seq") * head_count + lax.axis_index("head")
    upper = me // half
    spot = me % half

    def place(index):
        return (index // head_count, index % head_count)

    loads = [
        pltpu.make_async_copy(ref, outbound.at[i], local_sem.at[i])
        for i, ref in enumerate((k_ref, v_ref, q_ref, g_ref))
    ]
    for load in loads:
        load.start()

    barrier = pltpu.get_barrier_semaphore()

    def greet(step, carry):
        pl.semaphore_signal(
            barrier,
            inc=1,
            device_id=place((me + step) % devices),
            device_id_type=pl.DeviceIdType.MESH,
        )
        return carry

    lax.fori_loop(1, devices, greet, 0)

    @pl.when(upper == 0)
    def clear():
        inbound[:, 0:2, 0:half_rows, :] = jnp.zeros(
            (local_heads, 2, half_rows, DH), inbound.dtype
        )

    for load in loads:
        load.wait()
    pl.semaphore_wait(barrier, devices - 1)

    def near(step):
        return upper * half + (spot + 1 + step) % half

    def across(step):
        return (1 - upper) * half + (spot + 1 + step) % half

    def copy_in(head, peer, source):
        return pltpu.make_async_remote_copy(
            src_ref=outbound.at[:, :, rows_of((peer % half) * local_heads + head, DH)],
            dst_ref=inbound.at[head, :, rows_of(half + source % half, rows), :],
            send_sem=send_in.at[head, peer],
            recv_sem=recv_in.at[head, source],
            device_id=place(peer),
            device_id_type=pl.DeviceIdType.MESH,
        )

    def copy_up(head, peer, source):
        return pltpu.make_async_remote_copy(
            src_ref=outbound.at[0:2, :, rows_of((peer % half) * local_heads + head, DH)],
            dst_ref=inbound.at[head, 0:2, rows_of(source % half, rows), :],
            send_sem=send_in.at[head, peer],
            recv_sem=recv_in.at[head, source],
            device_id=place(peer),
            device_id_type=pl.DeviceIdType.MESH,
        )

    def copy_out(head, peer, source):
        return pltpu.make_async_remote_copy(
            src_ref=results.at[head, :, rows_of(peer % half, rows), :],
            dst_ref=landed.at[:, :, rows_of((source % half) * local_heads + head, DH)],
            send_sem=send_out.at[head, peer],
            recv_sem=recv_out.at[head, source],
            device_id=place(peer),
            device_id_type=pl.DeviceIdType.MESH,
        )

    def copy_back(head, peer, source):
        return pltpu.make_async_remote_copy(
            src_ref=results_back.at[head, :, rows_of(peer % half, rows), :],
            dst_ref=returned.at[:, :, rows_of((source % half) * local_heads + head, DH)],
            send_sem=send_out.at[head, peer],
            recv_sem=recv_out.at[head, source],
            device_id=place(peer),
            device_id_type=pl.DeviceIdType.MESH,
        )

    def own_in(head):
        return pltpu.make_async_copy(
            outbound.at[:, :, rows_of(spot * local_heads + head, DH)],
            inbound.at[head, :, rows_of(half + spot, rows), :],
            own_in_sem.at[head],
        )

    def own_out(head):
        return pltpu.make_async_copy(
            results.at[head, :, rows_of(spot, rows), :],
            landed.at[:, :, rows_of(spot * local_heads + head, DH)],
            own_out_sem.at[head],
        )

    def each(count, act):
        def step_of(step, carry):
            act(step)
            return carry

        lax.fori_loop(0, count, step_of, 0)

    for head in range(local_heads):

        @pl.when(upper == 0)
        def send_both():
            def two(step):
                copy_up(head, across(step), me).start()
                copy_in(head, near(step), me).start()

            each(half - 1, two)
            copy_up(head, across(half - 1), me).start()

        @pl.when(upper == 1)
        def send_near():
            each(half - 1, lambda step: copy_in(head, near(step), me).start())

        own_in(head).start()

    query_at = lax.broadcasted_iota(jnp.int32, (BLK, BLK), 0)
    key_at = lax.broadcasted_iota(jnp.int32, (BLK, BLK), 1)
    causal = key_at <= query_at

    def dot(a, b, dims):
        return lax.dot_general(a, b, (dims, ((), ())), preferred_element_type=jnp.float32)

    def attend(head, block):
        here = rows_of(block, BLK)
        own = rows_of(half_blocks + block, BLK)
        sources = [rows_of(half_blocks + block - offset, BLK) for offset in offsets]
        query = inbound[head, 2, own, :]
        grad = inbound[head, 3, own, :]
        keys = jnp.concatenate([inbound[head, 0, source, :] for source in sources], axis=0)
        values = jnp.concatenate([inbound[head, 1, source, :] for source in sources], axis=0)
        scores = dot(query, keys, ((1,), (1,))) * scale
        pieces = []
        for j in range(columns):
            live = mask_ref[j, upper * half_blocks + block] == 1
            piece = scores[:, j * BLK : (j + 1) * BLK]
            if j == 0:
                piece = jnp.where(causal, piece, NEG)
            pieces.append(jnp.where(live, piece, NEG))
        scores = jnp.concatenate(pieces, axis=1)
        row_max = jnp.max(scores, axis=1, keepdims=True)
        raised = jnp.exp(scores - row_max)
        total = jnp.sum(raised, axis=1, keepdims=True)
        weights = raised * (1.0 / total)
        rounded = weights.astype(jnp.bfloat16)
        attended = dot(rounded, values, ((1,), (0,))).astype(jnp.bfloat16)
        delta = jnp.sum(
            grad.astype(jnp.float32) * attended.astype(jnp.float32), axis=1, keepdims=True
        )
        grad_weights = dot(grad, values, ((1,), (1,)))
        grad_scores = (weights * (grad_weights - delta) * scale).astype(jnp.bfloat16)
        query_grad = dot(grad_scores, keys, ((1,), (0,))).astype(jnp.bfloat16)
        key_parts = dot(grad_scores, query, ((0,), (0,)))
        value_parts = dot(rounded, grad, ((0,), (0,)))
        results[head, 0, here, :] = attended
        results[head, 1, here, :] = query_grad
        key_sum[own, :] = key_parts[:BLK]
        value_sum[own, :] = value_parts[:BLK]
        for j in range(1, columns):
            piece = slice(j * BLK, (j + 1) * BLK)
            key_sum[sources[j], :] += key_parts[piece]
            value_sum[sources[j], :] += value_parts[piece]

    for head in range(local_heads):
        key_sum[0:half_rows, :] = jnp.zeros((half_rows, DH), jnp.float32)
        value_sum[0:half_rows, :] = jnp.zeros((half_rows, DH), jnp.float32)
        own_in(head).wait()
        each(half - 1, lambda step: copy_in(head, near(step), near(step)).wait_recv())

        @pl.when(upper == 1)
        def await_lower():
            each(half, lambda step: copy_up(head, across(step), across(step)).wait_recv())

        for block in range(half_blocks):
            attend(head, block)

        @pl.when(upper == 1)
        def send_back():
            results_back[head, 0] = key_sum[0:half_rows, :].astype(jnp.bfloat16)
            results_back[head, 1] = value_sum[0:half_rows, :].astype(jnp.bfloat16)
            each(half, lambda step: copy_back(head, across(step), me).start())

        results[head, 2] = key_sum[half_rows : 2 * half_rows, :].astype(jnp.bfloat16)
        results[head, 3] = value_sum[half_rows : 2 * half_rows, :].astype(jnp.bfloat16)
        each(half - 1, lambda step: copy_out(head, near(step), me).start())
        own_out(head).start()

    for head in range(local_heads):
        own_out(head).wait()

        def settle(step):
            peer = near(step)
            copy_in(head, peer, peer).wait_send()
            copy = copy_out(head, peer, peer)
            copy.wait_send()
            copy.wait_recv()

        each(half - 1, settle)

        @pl.when(upper == 0)
        def settle_lower():
            def one(step):
                peer = across(step)
                copy_up(head, peer, peer).wait_send()
                copy_back(head, peer, peer).wait_recv()

            each(half, one)

        @pl.when(upper == 1)
        def settle_upper():
            each(half, lambda step: copy_back(head, across(step), across(step)).wait_send())


def hand_out(seq_count, landed, returned, out_ref, dq_ref, dk_ref, dv_ref):
    lower = lax.axis_index("seq") < seq_count // 2
    out_ref[...] = landed[0]
    dq_ref[...] = landed[1]
    for i, ref in enumerate((dk_ref, dv_ref)):
        own = landed[2 + i]
        both = own.astype(jnp.float32) + returned[i].astype(jnp.float32)
        ref[...] = jnp.where(lower, both.astype(own.dtype), own)


def fused(seq_count, head_count, queries, key_vectors, value_vectors, out_cotangent, block_mask):
    devices = seq_count * head_count
    half = devices // 2
    rows, width = queries.shape
    tokens, local_heads = rows * devices, width // DH // half
    kind = queries.dtype
    anywhere = pl.BlockSpec(memory_space=pl.ANY)
    vmem = pl.BlockSpec(memory_space=pltpu.VMEM)
    one = jax.ShapeDtypeStruct((rows, width), kind)
    landed, returned = pl.pallas_call(
        functools.partial(fused_kernel, seq_count, head_count),
        out_shape=(
            jax.ShapeDtypeStruct((4, rows, width), kind),
            jax.ShapeDtypeStruct((2, rows, width), kind),
        ),
        in_specs=[pl.BlockSpec(memory_space=pltpu.SMEM)] + [anywhere] * 4,
        out_specs=(anywhere,) * 2,
        scratch_shapes=[
            pltpu.VMEM((4, rows, width), kind),
            pltpu.VMEM((local_heads, 4, tokens, DH), kind),
            pltpu.VMEM((local_heads, 4, tokens // 2, DH), kind),
            pltpu.VMEM((local_heads, 2, tokens // 2, DH), kind),
            pltpu.VMEM((tokens, DH), jnp.float32),
            pltpu.VMEM((tokens, DH), jnp.float32),
            pltpu.SemaphoreType.DMA((4,)),
            pltpu.SemaphoreType.DMA((local_heads,)),
            pltpu.SemaphoreType.DMA((local_heads,)),
            pltpu.SemaphoreType.DMA((local_heads, devices)),
            pltpu.SemaphoreType.DMA((local_heads, devices)),
            pltpu.SemaphoreType.DMA((local_heads, devices)),
            pltpu.SemaphoreType.DMA((local_heads, devices)),
        ],
        compiler_params=pltpu.CompilerParams(
            collective_id=0, has_side_effects=True, vmem_limit_bytes=62 * 1024 * 1024
        ),
    )(block_mask.T, queries, key_vectors, value_vectors, out_cotangent)
    return pl.pallas_call(
        functools.partial(hand_out, seq_count),
        out_shape=(one,) * 4,
        in_specs=[vmem] * 2,
        out_specs=(vmem,) * 4,
    )(landed, returned)


def per_device(seq_count, head_count, queries, key_vectors, value_vectors, out_cotangent, block_mask):
    heads = queries.shape[1] // DH
    devices = seq_count * head_count
    tokens = queries.shape[0] * devices
    blocks, columns = block_mask.shape
    halves = seq_count % 2 == 0 and blocks % 2 == 0 and tokens == blocks * BLK
    if halves and heads % (devices // 2) == 0 and 2 ** max(columns - 2, 0) <= blocks // 2:
        return fused(
            seq_count, head_count, queries, key_vectors, value_vectors, out_cotangent, block_mask
        )
    return shards(queries, key_vectors, value_vectors, out_cotangent, block_mask)


def solution(mesh):
    placed = (
        P(("seq", "head"), None),
        P(("seq", "head"), None),
        P(("seq", "head"), None),
        P(("seq", "head"), None),
        P(),
    )
    return jax.shard_map(
        functools.partial(per_device, mesh.shape["seq"], mesh.shape["head"]),
        mesh=mesh,
        in_specs=placed,
        out_specs=(
            P(("seq", "head"), None),
            P(("seq", "head"), None),
            P(("seq", "head"), None),
            P(("seq", "head"), None),
        ),
        check_vma=False,
    )
```
